32 devices in a mesh: seq: 8 (over z, x), tensor: 4 (over y, core).
Axes of the slice: x: 2, y: 2, z: 4, core: 2. Of those that a mesh axis runs over, the one named last changes fastest.
Arguments:
- history: bfloat16 [2, 2, 2048, 8192], P(None, None, 'seq', 'tensor'), may hold values from -6 to 6
- gates: bfloat16 [2, 2, 32, 8192], P(None, None, 'seq', 'tensor'), may hold values from -6 to 6
- rates: float32 [2, 16, 8192], P(None, None, 'tensor'), may hold values from 0.00014648438 to 0.1
- residues: float32 [2, 16, 8192], P(None, None, 'tensor'), may hold values from -2.1 to 2.1
- freqs: float32 [2, 16, 8192], P(None, None, 'tensor'), may hold values from 0 to 3.14159
- w_out: bfloat16 [2, 8192, 8192], P(None, 'tensor', 'seq'), may hold values from -0.0625 to 0.0625
- lengths: int32 [2], replicated, may hold values from 128 to 1536, as said below
- tile_index: int32 [1], replicated, may hold values from 0 to 15
Outputs:
- mixed: bfloat16 [2, 2, 32, 8192], P(None, None, 'tensor', 'seq')
The draws below stay inside these ranges and needn't reach their ends.
Inputs may be any that keep to these rules, and one draw needn't show every extreme that they name: `lengths`: each length is a multiple of 128; at least one genome has the largest length.
All inputs are finite; a program needn't handle non-finite values.
Results may differ from the reference program's by a relative error of at most 0.0049.
Values may be sent and summed in bfloat16 or wider, within the bound.
A program may use at most 64 MiB of HBM per device.

```python
import math
import jax
import jax.numpy as jnp
from jax import lax

D = 8192
MODES = 16
LAYERS = 2
UNIT = 128
AHEAD = 16
GENOMES = 2
LENGTH = 2048
TILE = 32


def draw_lengths(key, part):
    key = jax.random.fold_in(key, 5)
    top = (LENGTH - AHEAD * TILE) // UNIT
    first_key, second_key = jax.random.split(key)
    counts = jax.random.randint(first_key, (GENOMES,), 1, top)
    longest = jax.random.randint(second_key, (), 0, GENOMES)
    counts = jnp.where(jnp.arange(GENOMES) == longest, top, counts)
    return (counts * UNIT).astype(jnp.int32)


def levels(own_key, dims, shards, smallest, largest):
    factor_of = 1.0
    for position, blocks in shards:
        draws = jax.random.uniform(jax.random.fold_in(jax.random.fold_in(own_key, 6), position), (blocks,), jnp.float32, smallest / len(shards), largest / len(shards))
        factor_of = factor_of * jnp.repeat(jnp.exp(draws), dims[position] // blocks).reshape((-1,) + (1,) * (len(dims) - 1 - position))
    return factor_of


def bell_draw(rng, shape, spread, most, pieces=(), held_as=jnp.bfloat16):
    loudness = levels(rng, shape, pieces, -0.22, 0.18) if pieces else 1.0
    entries = jax.random.normal(rng, shape, jnp.float32) * spread * loudness
    return jnp.minimum(jnp.maximum(entries, -most), most).astype(held_as)


def setup_inputs(seed: int = 0) -> dict:
    key_list = jax.random.split(jax.random.key(seed), 9)
    return {
        "history": bell_draw(key_list[0], (LAYERS, GENOMES, LENGTH, D), 1.0, 6.0, ((2, 8), (3, 4))),
        "gates": bell_draw(key_list[1], (LAYERS, GENOMES, TILE, D), 1.0, 6.0, ((2, 8), (3, 4))),
        "rates": jnp.clip(jnp.exp(math.log(0.1) - 6.5260067 * jax.random.uniform(key_list[2], (LAYERS, MODES, D), jnp.float32) ** levels(key_list[2], (LAYERS, MODES, D), ((2, 4),), -0.2, 0.2)), 0.00014648438, 0.1),
        "residues": bell_draw(key_list[3], (LAYERS, MODES, D), 0.35, 2.1, ((2, 4),), jnp.float32),
        "freqs": jnp.clip(3.14159 * jax.random.uniform(key_list[4], (LAYERS, MODES, D), jnp.float32) ** levels(key_list[4], (LAYERS, MODES, D), ((2, 4),), -0.2, 0.2), 0.0, 3.14159),
        "w_out": bell_draw(key_list[5], (LAYERS, D, D), D ** -0.5, 0.0625, ((1, 4), (2, 8))),
        "lengths": draw_lengths(jax.random.fold_in(key_list[8], 71), 0),
        "tile_index": jax.random.randint(key_list[7], (1,), 0, AHEAD).astype(jnp.int32),
    }


def lag_states(x_g, t0, positions, rate, freq):
    lag = t0 - positions
    live = lag > 0
    steps = jnp.where(live, lag, 0).astype(jnp.int32)
    steps_f = steps.astype(jnp.float32)
    values = jnp.where(live[:, None], x_g.astype(jnp.float32), jnp.float32(0.0))
    chans = values.shape[1]
    width = min(chans, 128)
    count = chans // width
    blocks_x = values.reshape(values.shape[0], count, width).transpose(1, 0, 2)
    blocks_r = rate.reshape(rate.shape[0], count, width).transpose(1, 0, 2)
    blocks_f = freq.reshape(freq.shape[0], count, width).transpose(1, 0, 2)

    def per_block(item):
        xb, rb, fb = item
        decay = jnp.exp(-rb[None, :, :] * steps_f[:, None, None])
        angle = fb[None, :, :] * steps_f[:, None, None]
        scaled = decay * xb[:, None, :]
        return (lax.optimization_barrier(jnp.sum(scaled * jnp.cos(angle), axis=0)), lax.optimization_barrier(jnp.sum(scaled * jnp.sin(angle), axis=0)))
    real_part, imag_part = lax.map(per_block, (blocks_x, blocks_r, blocks_f))
    real_part = real_part.transpose(1, 0, 2).reshape(rate.shape[0], chans)
    imag_part = imag_part.transpose(1, 0, 2).reshape(rate.shape[0], chans)
    return (real_part, imag_part)

def row_tables(rate, resid, freq, rows):
    rows_f = rows.astype(jnp.float32)
    amplitude = resid[None] * jnp.sqrt(rate)[None] * jnp.exp(-rate[None] * rows_f[:, None, None])
    angle = freq[None] * rows_f[:, None, None]
    return (amplitude * jnp.cos(angle), amplitude * jnp.sin(angle))

def reference(history, gates, rates, residues, freqs, w_out, lengths, tile_index):
    flush_at = (lengths + TILE * tile_index[0]).astype(jnp.int32)
    positions = jnp.arange(LENGTH, dtype=jnp.int32)
    rows = jnp.arange(TILE, dtype=jnp.int32)
    outputs = []
    for layer in range(LAYERS):
        rate = rates[layer]
        freq = freqs[layer]

        def genome_states(item):
            return lag_states(item[0], item[1], positions, rate, freq)
        real_part, imag_part = lax.map(genome_states, (history[layer], flush_at))
        table_re, table_im = row_tables(rate, residues[layer], freq, rows)
        contrib = jnp.einsum('jmc,gmc->gjc', table_re, real_part, precision=lax.Precision.HIGHEST)
        contrib = contrib - jnp.einsum('jmc,gmc->gjc', table_im, imag_part, precision=lax.Precision.HIGHEST)
        gated = (contrib * gates[layer].astype(jnp.float32)).astype(jnp.bfloat16)
        flat = gated.reshape(GENOMES * TILE, D)
        mixed = jnp.dot(flat, w_out[layer], preferred_element_type=jnp.float32).astype(jnp.bfloat16)
        outputs.append(mixed.reshape(GENOMES, TILE, D))
    return jnp.stack(outputs, axis=0)
```

```python
import functools
import math

import jax
import jax.numpy as jnp
from jax import lax
from jax.experimental import pallas as pl
from jax.experimental.pallas import tpu as pltpu
from jax.sharding import PartitionSpec as P

UNIT = 128
SUB = 8
LANE = 128
GROUP = 4
STEPS = 64
RUN = 32


def cmul(ar, ai, br, bi):
    return ar * br - ai * bi, ar * bi + ai * br


def csq(ar, ai):
    return ar * ar - ai * ai, 2.0 * (ar * ai)


def cos_sin(angle):
    y = (angle - 1.57079637050628662) + 4.37113883e-8
    y2 = y * y
    s = jnp.full_like(y, 1.0 / math.factorial(13))
    for n, sign in ((11, -1), (9, 1), (7, -1), (5, 1), (3, -1), (1, 1)):
        s = s * y2 + sign / math.factorial(n)
    c = jnp.full_like(y, -1.0 / math.factorial(14))
    for n, sign in ((12, 1), (10, -1), (8, 1), (6, -1), (4, 1), (2, -1), (0, 1)):
        c = c * y2 + sign / math.factorial(n)
    return -(s * y), c


def spread_rows(dst, base, value):
    count = value.shape[0]
    for k in range(SUB):
        dst[pl.ds(base + k, count, stride=SUB), :] = value[:, k * LANE:(k + 1) * LANE]


def local_kernel(granule, bits, info, x_ref, rate_ref, resid_ref, freq_ref, out_ref, xs, pars):
    genomes, span = x_ref.shape[1], x_ref.shape[2]
    modes = rate_ref.shape[1]
    rows = out_ref.shape[1]
    chunk = 32
    first = info[genomes]
    for i, ref in enumerate((rate_ref, resid_ref, freq_ref)):
        spread_rows(pars.at[i], 0, ref[0])
    hops = []
    for g in range(genomes):
        live = jnp.minimum(jnp.maximum(info[g] - first, 0), span)
        hops.append(lax.div(jnp.maximum(info[g] - first - live, 0), granule))

        @pl.loop(0, span // chunk)
        def _(q):
            src = q * chunk - (span - live)
            block = x_ref[0, g, pl.ds(pl.multiple_of(jnp.maximum(src, 0), chunk), chunk), :]
            block = jnp.where(src >= 0, block.astype(jnp.float32), 0.0)
            spread_rows(xs.at[g], q * (chunk * SUB), block)

    out_ref[...] = jnp.zeros_like(out_ref)
    wide = GROUP * SUB

    @pl.loop(0, modes // GROUP)
    def _(mg):
        at = pl.ds(pl.multiple_of(mg * wide, wide), wide)
        rate, resid, freq = pars[0, at, :], pars[1, at, :], pars[2, at, :]
        decay = jnp.exp(-rate)
        c, s = cos_sin(freq)
        zr, zi = decay * c, decay * s
        trace, norm = 2.0 * zr, zr * zr + zi * zi
        amp = resid * jnp.sqrt(rate)

        def cut(v):
            return [v[i * SUB:(i + 1) * SUB] for i in range(GROUP)]

        zr_c, zi_c, tr_c, no_c = cut(zr), cut(zi), cut(trace), cut(norm)
        pr, pi = zr, zi
        for _ in range(int(math.log2(STEPS))):
            pr, pi = csq(pr, pi)
        br_c, bi_c = cut(pr), cut(pi)
        n_state = genomes * GROUP
        zero = jnp.zeros((SUB, LANE), jnp.float32)

        def block_step(blk, carry):
            re, im = carry
            a = [zero] * n_state
            b = [zero] * n_state
            for t in range(STEPS):
                for g in range(genomes):
                    x = xs[g, pl.ds(pl.multiple_of(blk * (STEPS * SUB) + t * SUB, SUB), SUB), :]
                    for i in range(GROUP):
                        k = g * GROUP + i
                        a[k], b[k] = b[k] + tr_c[i] * a[k], x - no_c[i] * a[k]
            new_re, new_im = [], []
            for g in range(genomes):
                for i in range(GROUP):
                    k = g * GROUP + i
                    sr, si = cmul(br_c[i], bi_c[i], re[k], im[k])
                    new_re.append(sr + (zr_c[i] * a[k] + b[k]))
                    new_im.append(si + zi_c[i] * a[k])
            return tuple(new_re), tuple(new_im)

        init = ((zero,) * n_state, (zero,) * n_state)
        re, im = lax.fori_loop(0, span // STEPS, block_step, init)

        pr, pi = zr, zi
        for _ in range(int(math.log2(granule))):
            pr, pi = csq(pr, pi)
        lead_r, lead_i = amp * zr, amp * zi
        far = [(lead_r, lead_i) for _ in range(genomes)]
        for bit in range(bits):
            for g in range(genomes):
                fr, fi = far[g]
                nr, ni = cmul(fr, fi, pr, pi)
                on = lax.rem(lax.div(hops[g], 1 << bit), 2) == 1
                far[g] = (jnp.where(on, nr, fr), jnp.where(on, ni, fi))
            if bit + 1 < bits:
                pr, pi = csq(pr, pi)
        start = []
        for g in range(genomes):
            fr, fi = cut(far[g][0]), cut(far[g][1])
            start.append([cmul(re[g * GROUP + i], im[g * GROUP + i], fr[i], fi[i]) for i in range(GROUP)])
        qr, qi = zr, zi
        for _ in range(int(math.log2(RUN))):
            qr, qi = csq(qr, qi)
        qr_c, qi_c = cut(qr), cut(qi)

        def row_run(run, carry):
            wr, wi = carry
            base = run * RUN
            old = [None] * n_state
            now = list(wr)
            for j in range(RUN):
                for g in range(genomes):
                    total = now[g * GROUP]
                    for i in range(1, GROUP):
                        total = total + now[g * GROUP + i]
                    out_ref[0, base + j, g] += total
                for g in range(genomes):
                    for i in range(GROUP):
                        k = g * GROUP + i
                        if j == 0:
                            nxt = wr[k] * zr_c[i] - wi[k] * zi_c[i]
                        else:
                            nxt = tr_c[i] * now[k] - no_c[i] * old[k]
                        old[k], now[k] = now[k], nxt
            moved = [cmul(wr[g * GROUP + i], wi[g * GROUP + i], qr_c[i], qi_c[i])
                     for g in range(genomes) for i in range(GROUP)]
            return tuple(m[0] for m in moved), tuple(m[1] for m in moved)

        wr = tuple(start[g][i][0] for g in range(genomes) for i in range(GROUP))
        wi = tuple(start[g][i][1] for g in range(genomes) for i in range(GROUP))
        lax.fori_loop(0, rows // RUN, row_run, (wr, wi))


def local_terms(info, history, rates, residues, freqs, rows, bits, granule):
    layers, genomes, span, chans = history.shape
    modes = rates.shape[1]
    wide = SUB * LANE
    par_spec = pl.BlockSpec((1, modes, wide), lambda l, c: (l, 0, c))
    return pl.pallas_call(
        functools.partial(local_kernel, granule, bits),
        grid=(layers, chans // wide),
        out_shape=jax.ShapeDtypeStruct((layers, rows, genomes, chans // LANE, LANE), jnp.float32),
        in_specs=[
            pl.BlockSpec(memory_space=pltpu.SMEM),
            pl.BlockSpec((1, genomes, span, wide), lambda l, c: (l, 0, 0, c)),
            par_spec, par_spec, par_spec,
        ],
        out_specs=pl.BlockSpec((1, rows, genomes, SUB, LANE), lambda l, c: (l, 0, 0, c, 0)),
        scratch_shapes=[
            pltpu.VMEM((genomes, span * SUB, LANE), jnp.float32),
            pltpu.VMEM((3, modes * SUB, LANE), jnp.float32),
        ],
        compiler_params=pltpu.CompilerParams(vmem_limit_bytes=48 * 1024 * 1024),
    )(info, history, rates, residues, freqs)


def shards(history, gates, rates, residues, freqs, w_out, lengths, tile_index):
    layers, genomes, span, chans = history.shape
    rows_dev = gates.shape[2]
    seq_size = lax.axis_size("seq")
    tile = rows_dev * seq_size
    granule = math.gcd(UNIT, tile)
    bits = (span * seq_size // granule).bit_length()
    flush_at = lengths + tile * tile_index[0]
    first = lax.axis_index("seq") * span
    info = jnp.concatenate([flush_at, first[None]]).astype(jnp.int32)
    term = local_terms(info, history, rates, residues, freqs, tile, bits, granule)
    summed = lax.psum_scatter(term, "seq", scatter_dimension=1, tiled=True)
    gates_t = gates.transpose(0, 2, 1, 3).astype(jnp.float32)
    gated = (summed.reshape(layers, rows_dev, genomes, chans) * gates_t).astype(jnp.bfloat16)
    full = lax.all_gather(gated, "seq", axis=1, tiled=True)
    partial_out = jnp.einsum("ljgc,lcd->lgjd", full, w_out, preferred_element_type=jnp.float32)
    mixed = lax.psum_scatter(partial_out, "tensor", scatter_dimension=2, tiled=True)
    return mixed.astype(jnp.bfloat16)


def solution(mesh):
    in_specs = (
        P(None, None, "seq", "tensor"),
        P(None, None, "seq", "tensor"),
        P(None, None, "tensor"),
        P(None, None, "tensor"),
        P(None, None, "tensor"),
        P(None, "tensor", "seq"),
        P(),
        P(),
    )
    out_specs = P(None, None, "tensor", "seq")
    return jax.shard_map(shards, mesh=mesh, in_specs=in_specs, out_specs=out_specs, check_vma=False)
```

```python
import functools
import math

import jax
import jax.numpy as jnp
from jax import lax
from jax.experimental import pallas as pl
from jax.experimental.pallas import tpu as pltpu
from jax.sharding import PartitionSpec as P

MESH = pl.DeviceIdType.MESH
UNIT = 128
SUB = 8
LANE = 128
GROUP = 4
STEPS = 64
RUN = 32


def cmul(ar, ai, br, bi):
    return ar * br - ai * bi, ar * bi + ai * br


def csq(ar, ai):
    return ar * ar - ai * ai, 2.0 * (ar * ai)


def cos_sin(angle):
    y = (angle - 1.57079637050628662) + 4.37113883e-8
    y2 = y * y
    s = jnp.full_like(y, 1.0 / math.factorial(13))
    for n, sign in ((11, -1), (9, 1), (7, -1), (5, 1), (3, -1), (1, 1)):
        s = s * y2 + sign / math.factorial(n)
    c = jnp.full_like(y, -1.0 / math.factorial(14))
    for n, sign in ((12, 1), (10, -1), (8, 1), (6, -1), (4, 1), (2, -1), (0, 1)):
        c = c * y2 + sign / math.factorial(n)
    return -(s * y), c


def spread_rows(dst, base, value):
    count = value.shape[0]
    for k in range(SUB):
        dst[pl.ds(base + k, count, stride=SUB), :] = value[:, k * LANE:(k + 1) * LANE]


def local_kernel(granule, bits, info, x_ref, rate_ref, resid_ref, freq_ref, out_ref, xs, pars, acc):
    genomes, span = x_ref.shape[1], x_ref.shape[2]
    modes = rate_ref.shape[1]
    rows = acc.shape[1]
    chunk = 32
    first = info[genomes]
    for i, ref in enumerate((rate_ref, resid_ref, freq_ref)):
        spread_rows(pars.at[i], 0, ref[0])
    hops = []
    for g in range(genomes):
        live = jnp.minimum(jnp.maximum(info[g] - first, 0), span)
        hops.append(lax.div(jnp.maximum(info[g] - first - live, 0), granule))

        @pl.loop(0, span // chunk)
        def _(q):
            src = q * chunk - (span - live)
            block = x_ref[0, g, pl.ds(pl.multiple_of(jnp.maximum(src, 0), chunk), chunk), :]
            block = jnp.where(src >= 0, block.astype(jnp.float32), 0.0)
            spread_rows(xs.at[g], q * (chunk * SUB), block)

    acc[...] = jnp.zeros_like(acc)
    wide = GROUP * SUB

    @pl.loop(0, modes // GROUP)
    def _(mg):
        at = pl.ds(pl.multiple_of(mg * wide, wide), wide)
        rate, resid, freq = pars[0, at, :], pars[1, at, :], pars[2, at, :]
        decay = jnp.exp(-rate)
        c, s = cos_sin(freq)
        zr, zi = decay * c, decay * s
        trace, norm = 2.0 * zr, zr * zr + zi * zi
        amp = resid * jnp.sqrt(rate)

        def cut(v):
            return [v[i * SUB:(i + 1) * SUB] for i in range(GROUP)]

        zr_c, zi_c, tr_c, no_c = cut(zr), cut(zi), cut(trace), cut(norm)
        pr, pi = zr, zi
        for _ in range(int(math.log2(STEPS))):
            pr, pi = csq(pr, pi)
        br_c, bi_c = cut(pr), cut(pi)
        n_state = genomes * GROUP
        zero = jnp.zeros((SUB, LANE), jnp.float32)

        def block_step(blk, carry):
            re, im = carry
            a = [zero] * n_state
            b = [zero] * n_state
            for t in range(STEPS):
                for g in range(genomes):
                    x = xs[g, pl.ds(pl.multiple_of(blk * (STEPS * SUB) + t * SUB, SUB), SUB), :]
                    for i in range(GROUP):
                        k = g * GROUP + i
                        a[k], b[k] = b[k] + tr_c[i] * a[k], x - no_c[i] * a[k]
            new_re, new_im = [], []
            for g in range(genomes):
                for i in range(GROUP):
                    k = g * GROUP + i
                    sr, si = cmul(br_c[i], bi_c[i], re[k], im[k])
                    new_re.append(sr + (zr_c[i] * a[k] + b[k]))
                    new_im.append(si + zi_c[i] * a[k])
            return tuple(new_re), tuple(new_im)

        init = ((zero,) * n_state, (zero,) * n_state)
        re, im = lax.fori_loop(0, span // STEPS, block_step, init)

        pr, pi = zr, zi
        for _ in range(int(math.log2(granule))):
            pr, pi = csq(pr, pi)
        lead_r, lead_i = amp * zr, amp * zi
        far = [(lead_r, lead_i) for _ in range(genomes)]
        for bit in range(bits):
            for g in range(genomes):
                fr, fi = far[g]
                nr, ni = cmul(fr, fi, pr, pi)
                on = lax.rem(lax.div(hops[g], 1 << bit), 2) == 1
                far[g] = (jnp.where(on, nr, fr), jnp.where(on, ni, fi))
            if bit + 1 < bits:
                pr, pi = csq(pr, pi)
        start = []
        for g in range(genomes):
            fr, fi = cut(far[g][0]), cut(far[g][1])
            start.append([cmul(re[g * GROUP + i], im[g * GROUP + i], fr[i], fi[i]) for i in range(GROUP)])
        qr, qi = zr, zi
        for _ in range(int(math.log2(RUN))):
            qr, qi = csq(qr, qi)
        qr_c, qi_c = cut(qr), cut(qi)

        def row_run(run, carry):
            wr, wi = carry
            base = run * RUN
            old = [None] * n_state
            now = list(wr)
            for j in range(RUN):
                for g in range(genomes):
                    total = now[g * GROUP]
                    for i in range(1, GROUP):
                        total = total + now[g * GROUP + i]
                    acc[g, base + j] += total
                for g in range(genomes):
                    for i in range(GROUP):
                        k = g * GROUP + i
                        if j == 0:
                            nxt = wr[k] * zr_c[i] - wi[k] * zi_c[i]
                        else:
                            nxt = tr_c[i] * now[k] - no_c[i] * old[k]
                        old[k], now[k] = now[k], nxt
            moved = [cmul(wr[g * GROUP + i], wi[g * GROUP + i], qr_c[i], qi_c[i])
                     for g in range(genomes) for i in range(GROUP)]
            return tuple(m[0] for m in moved), tuple(m[1] for m in moved)

        wr = tuple(start[g][i][0] for g in range(genomes) for i in range(GROUP))
        wi = tuple(start[g][i][1] for g in range(genomes) for i in range(GROUP))
        lax.fori_loop(0, rows // RUN, row_run, (wr, wi))

    out_ref[0, 0] = acc[...].reshape(out_ref.shape[2:]).astype(out_ref.dtype)


def local_terms(info, history, rates, residues, freqs, rows_dev, seq_size, bits, granule):
    layers, genomes, span, chans = history.shape
    modes = rates.shape[1]
    wide = SUB * LANE
    rows = rows_dev * seq_size
    par_spec = pl.BlockSpec((1, modes, wide), lambda l, c: (l, 0, c))
    piece = (genomes, seq_size, rows_dev // 2, 2 * SUB, LANE)
    return pl.pallas_call(
        functools.partial(local_kernel, granule, bits),
        grid=(layers, chans // wide),
        out_shape=jax.ShapeDtypeStruct((layers, chans // wide) + piece, jnp.bfloat16),
        in_specs=[
            pl.BlockSpec(memory_space=pltpu.SMEM),
            pl.BlockSpec((1, genomes, span, wide), lambda l, c: (l, 0, 0, c)),
            par_spec, par_spec, par_spec,
        ],
        out_specs=pl.BlockSpec((1, 1) + piece, lambda l, c: (l, c, 0, 0, 0, 0, 0)),
        scratch_shapes=[
            pltpu.VMEM((genomes, span * SUB, LANE), jnp.float32),
            pltpu.VMEM((3, modes * SUB, LANE), jnp.float32),
            pltpu.VMEM((genomes, rows, SUB, LANE), jnp.float32),
        ],
        compiler_params=pltpu.CompilerParams(vmem_limit_bytes=60 * 1024 * 1024),
    )(info, history, rates, residues, freqs)


def exchange_kernel(seq, tensor, term, gates, w_hbm, out, w, w_sem, got, flat, full, part, got2, s1, r1, s2, r2, s3, r3):
    me, tm = lax.axis_index("seq"), lax.axis_index("tensor")
    layers, blocks, genomes = term.shape[:3]
    own_rows = gates.shape[0]
    cols = w.shape[2]
    barrier = pltpu.get_barrier_semaphore()
    for k in range(1, seq):
        pl.semaphore_signal(barrier, inc=1, device_id={"seq": lax.rem(me + k, seq)}, device_id_type=MESH)
    for k in range(1, tensor):
        pl.semaphore_signal(barrier, inc=1, device_id={"tensor": lax.rem(tm + k, tensor)}, device_id_type=MESH)
    fetch = pltpu.make_async_copy(w_hbm, w, w_sem)
    fetch.start()
    pl.semaphore_wait(barrier, seq + tensor - 2)

    first = []
    for k in range(1, seq):
        peer = lax.rem(me + k, seq)
        copy = pltpu.make_async_remote_copy(
            src_ref=term.at[:, :, :, peer], dst_ref=got.at[k], send_sem=s1.at[k], recv_sem=r1.at[k],
            device_id={"seq": peer}, device_id_type=MESH)
        copy.start()
        first.append(copy)
    flat_shape = (own_rows // layers // genomes * SUB, LANE)
    for copy in first:
        copy.wait_recv()
    for l in range(layers):
        for c in range(blocks):
            for g in range(genomes):
                total = term[l, c, g, me].astype(jnp.float32)
                for k in range(1, seq):
                    total = total + got[k, l, c, g].astype(jnp.float32)
                flat[c, pl.ds((l * genomes + g) * flat_shape[0], flat_shape[0]), :] = total.reshape(flat_shape)
    for c in range(blocks):
        for k in range(SUB):
            at = pl.ds((c * SUB + k) * LANE, LANE)
            value = flat[c, pl.ds(k, own_rows, stride=SUB), :] * gates[:, at].astype(jnp.float32)
            full[me, :, at] = value.astype(full.dtype)

    second = []
    for k in range(1, seq):
        copy = pltpu.make_async_remote_copy(
            src_ref=full.at[me], dst_ref=full.at[me], send_sem=s2.at[k], recv_sem=r2.at[k],
            device_id={"seq": lax.rem(me + k, seq)}, device_id_type=MESH)
        copy.start()
        second.append(copy)
    fetch.wait()
    for k in range(1, seq):
        src = lax.rem(me - k + seq, seq)
        pltpu.make_async_remote_copy(
            src_ref=full.at[src], dst_ref=full.at[src], send_sem=s2.at[k], recv_sem=r2.at[k],
            device_id={"seq": lax.rem(me + k, seq)}, device_id_type=MESH).wait_recv()

    share = seq // tensor
    wide = part.shape[3]
    per = tensor if seq * own_rows <= 256 else 1
    third = []
    for n in range(cols // wide):
        @pl.loop(0, tensor // per)
        def _(t):
            block = full[pl.ds(t * (per * share), per * share)].reshape(per * share * own_rows, full.shape[2])
            both = [jnp.dot(block, w[l, :, n * wide:(n + 1) * wide], preferred_element_type=jnp.float32)
                    for l in range(layers)]
            at = lax.broadcasted_iota(jnp.int32, both[0].shape, 0)
            owner = lax.rem(at, own_rows) // (own_rows // layers)
            value = both[0]
            for l in range(1, layers):
                value = jnp.where(owner == l, both[l], value)
            part[n, pl.ds(t * per, per)] = value.reshape(per, share * own_rows, wide)
        for k in range(1, tensor):
            peer = lax.rem(tm + k, tensor)
            copy = pltpu.make_async_remote_copy(
                src_ref=part.at[n, peer], dst_ref=got2.at[n, k], send_sem=s3.at[n, k], recv_sem=r3.at[n, k],
                device_id={"tensor": peer}, device_id_type=MESH)
            copy.start()
            third.append(copy)
    for n in range(cols // wide):
        total = part[n, tm]
        for k in range(1, tensor):
            third[n * (tensor - 1) + k - 1].wait_recv()
            total = total + got2[n, k]
        out[:, n * wide:(n + 1) * wide] = total.astype(out.dtype)
    for copy in first + second + third:
        copy.wait_send()


def exchange(term, gates, w_out, seq, tensor):
    own_rows, chans = gates.shape
    layers, _, cols = w_out.shape
    wide = min(cols, 256)
    share = seq // tensor
    vmem = pl.BlockSpec(memory_space=pltpu.VMEM)
    return pl.pallas_call(
        functools.partial(exchange_kernel, seq, tensor),
        out_shape=jax.ShapeDtypeStruct((share * own_rows, cols), jnp.bfloat16),
        in_specs=[vmem, vmem, pl.BlockSpec(memory_space=pl.ANY)],
        out_specs=vmem,
        scratch_shapes=[
            pltpu.VMEM(w_out.shape, w_out.dtype),
            pltpu.SemaphoreType.DMA,
            pltpu.VMEM((seq,) + term.shape[:3] + term.shape[4:], term.dtype),
            pltpu.VMEM((term.shape[1], own_rows * SUB, LANE), jnp.float32),
            pltpu.VMEM((seq, own_rows, chans), jnp.bfloat16),
            pltpu.VMEM((cols // wide, tensor, share * own_rows, wide), jnp.float32),
            pltpu.VMEM((cols // wide, tensor, share * own_rows, wide), jnp.float32),
            pltpu.SemaphoreType.DMA((seq,)),
            pltpu.SemaphoreType.DMA((seq,)),
            pltpu.SemaphoreType.DMA((seq,)),
            pltpu.SemaphoreType.DMA((seq,)),
            pltpu.SemaphoreType.DMA((cols // wide, tensor)),
            pltpu.SemaphoreType.DMA((cols // wide, tensor)),
        ],
        compiler_params=pltpu.CompilerParams(
            collective_id=0, has_side_effects=True, vmem_limit_bytes=60 * 1024 * 1024),
    )(term, gates, w_out)


def shards(history, gates, rates, residues, freqs, w_out, lengths, tile_index):
    layers, genomes, span, chans = history.shape
    rows_dev = gates.shape[2]
    seq_size, tensor_size = lax.axis_size("seq"), lax.axis_size("tensor")
    tile = rows_dev * seq_size
    granule = math.gcd(UNIT, tile)
    bits = (span * seq_size // granule).bit_length()
    flush_at = lengths + tile * tile_index[0]
    first = lax.axis_index("seq") * span
    info = jnp.concatenate([flush_at, first[None]]).astype(jnp.int32)
    term = local_terms(info, history, rates, residues, freqs, rows_dev, seq_size, bits, granule)
    own_rows = layers * genomes * rows_dev
    mixed = exchange(term, gates.reshape(own_rows, chans), w_out, seq_size, tensor_size)
    share = seq_size // tensor_size
    mixed = mixed.reshape(share, layers, genomes, rows_dev, -1).transpose(1, 2, 0, 3, 4)
    return mixed.reshape(layers, genomes, share * rows_dev, -1)


def solution(mesh):
    in_specs = (
        P(None, None, "seq", "tensor"),
        P(None, None, "seq", "tensor"),
        P(None, None, "tensor"),
        P(None, None, "tensor"),
        P(None, None, "tensor"),
        P(None, "tensor", "seq"),
        P(),
        P(),
    )
    out_specs = P(None, None, "tensor", "seq")
    return jax.shard_map(shards, mesh=mesh, in_specs=in_specs, out_specs=out_specs, check_vma=False)
```

```python
import functools
import math

import jax
import jax.numpy as jnp
from jax import lax
from jax.experimental import pallas as pl
from jax.experimental.pallas import tpu as pltpu
from jax.sharding import PartitionSpec as P

MESH = pl.DeviceIdType.MESH
UNIT = 128
SUB = 8
LANE = 128
GROUP = 4
STEPS = 32
RUN = 32


def cmul(ar, ai, br, bi):
    return ar * br - ai * bi, ar * bi + ai * br


def csq(ar, ai):
    return ar * ar - ai * ai, 2.0 * (ar * ai)


def cos_sin(angle):
    y = (angle - 1.57079637050628662) + 4.37113883e-8
    y2 = y * y
    s = jnp.full_like(y, 1.0 / math.factorial(13))
    for n, sign in ((11, -1), (9, 1), (7, -1), (5, 1), (3, -1), (1, 1)):
        s = s * y2 + sign / math.factorial(n)
    c = jnp.full_like(y, -1.0 / math.factorial(14))
    for n, sign in ((12, 1), (10, -1), (8, 1), (6, -1), (4, 1), (2, -1), (0, 1)):
        c = c * y2 + sign / math.factorial(n)
    return -(s * y), c


def spread_rows(dst, base, value):
    count = value.shape[0]
    for k in range(SUB):
        dst[pl.ds(base + k, count, stride=SUB), :] = value[:, k * LANE:(k + 1) * LANE]


def local_step(granule, bits, first, starts, x_ref, params, l, c, acc, xs, pars):
    genomes, span = x_ref.shape[:2]
    modes = params[0].shape[1]
    rows = acc.shape[1]
    chunk = 32
    wide_cols = SUB * LANE
    for i, ref in enumerate(params):
        spread_rows(pars.at[i], 0, ref[l, :, pl.ds(pl.multiple_of(c * wide_cols, wide_cols), wide_cols)])
    hops, blocks_live = [], []
    for g in range(genomes):
        ahead = jnp.full((SUB, LANE), starts[g] - first, jnp.int32)
        live = jnp.minimum(jnp.maximum(ahead, 0), span)
        blocks_live.append(live)
        hops.append(jnp.maximum(ahead - live, 0))

        @pl.loop(0, span // chunk)
        def _(q):
            block = x_ref[g, pl.ds(pl.multiple_of(q * chunk, chunk), chunk), :]
            spread_rows(xs.at[g], q * (chunk * SUB), block.astype(jnp.float32))

    acc[...] = jnp.zeros_like(acc)
    wide = GROUP * SUB

    @pl.loop(0, modes // GROUP)
    def _(mg):
        at = pl.ds(pl.multiple_of(mg * wide, wide), wide)
        rate, resid, freq = pars[0, at, :], pars[1, at, :], pars[2, at, :]
        decay = jnp.exp(-rate)
        c, s = cos_sin(freq)
        zr, zi = decay * c, decay * s
        trace, norm = 2.0 * zr, zr * zr + zi * zi
        amp = resid * jnp.sqrt(rate)

        def cut(v):
            return [v[i * SUB:(i + 1) * SUB] for i in range(GROUP)]

        zr_c, zi_c, tr_c, no_c = cut(zr), cut(zi), cut(trace), cut(norm)
        pr, pi = zr, zi
        for _ in range(int(math.log2(STEPS))):
            pr, pi = csq(pr, pi)
        br_c, bi_c = cut(pr), cut(pi)
        n_state = genomes * GROUP
        zero = jnp.zeros((SUB, LANE), jnp.float32)

        def block_step(blk, carry):
            re, im = carry
            a = [zero] * n_state
            b = [zero] * n_state
            for t in range(STEPS):
                for g in range(genomes):
                    x = xs[g, pl.ds(pl.multiple_of(blk * (STEPS * SUB) + t * SUB, SUB), SUB), :]
                    for i in range(GROUP):
                        k = g * GROUP + i
                        a[k], b[k] = b[k] + tr_c[i] * a[k], x - no_c[i] * a[k]
            new_re, new_im = [], []
            for g in range(genomes):
                for i in range(GROUP):
                    k = g * GROUP + i
                    sr, si = cmul(br_c[i], bi_c[i], re[k], im[k])
                    keep = blocks_live[g] > blk * STEPS
                    new_re.append(jnp.where(keep, sr + (zr_c[i] * a[k] + b[k]), re[k]))
                    new_im.append(jnp.where(keep, si + zi_c[i] * a[k], im[k]))
            return tuple(new_re), tuple(new_im)

        init = ((zero,) * n_state, (zero,) * n_state)
        re, im = lax.fori_loop(0, span // STEPS, block_step, init)

        pr, pi = zr, zi
        for _ in range(int(math.log2(granule))):
            pr, pi = csq(pr, pi)
        lead_r, lead_i = amp * zr, amp * zi
        far_r = [cut(lead_r) for _ in range(genomes)]
        far_i = [cut(lead_i) for _ in range(genomes)]
        for bit in range(bits):
            pr_c, pi_c = cut(pr), cut(pi)
            for g in range(genomes):
                on = (hops[g] & (granule << bit)) != 0
                for i in range(GROUP):
                    nr, ni = cmul(far_r[g][i], far_i[g][i], pr_c[i], pi_c[i])
                    far_r[g][i] = jnp.where(on, nr, far_r[g][i])
                    far_i[g][i] = jnp.where(on, ni, far_i[g][i])
            if bit + 1 < bits:
                pr, pi = csq(pr, pi)
        start = []
        for g in range(genomes):
            fr, fi = far_r[g], far_i[g]
            start.append([cmul(re[g * GROUP + i], im[g * GROUP + i], fr[i], fi[i]) for i in range(GROUP)])
        qr, qi = zr, zi
        for _ in range(int(math.log2(RUN))):
            qr, qi = csq(qr, qi)
        qr_c, qi_c = cut(qr), cut(qi)

        def row_run(run, carry):
            wr, wi = carry
            base = run * RUN
            old = [None] * n_state
            now = list(wr)
            for j in range(RUN):
                for g in range(genomes):
                    total = now[g * GROUP]
                    for i in range(1, GROUP):
                        total = total + now[g * GROUP + i]
                    acc[g, base + j] += total
                for g in range(genomes):
                    for i in range(GROUP):
                        k = g * GROUP + i
                        if j == 0:
                            nxt = wr[k] * zr_c[i] - wi[k] * zi_c[i]
                        else:
                            nxt = tr_c[i] * now[k] - no_c[i] * old[k]
                        old[k], now[k] = now[k], nxt
            moved = [cmul(wr[g * GROUP + i], wi[g * GROUP + i], qr_c[i], qi_c[i])
                     for g in range(genomes) for i in range(GROUP)]
            return tuple(m[0] for m in moved), tuple(m[1] for m in moved)

        wr = tuple(start[g][i][0] for g in range(genomes) for i in range(GROUP))
        wi = tuple(start[g][i][1] for g in range(genomes) for i in range(GROUP))
        lax.fori_loop(0, rows // RUN, row_run, (wr, wi))


def kernel(seq, tensor, granule, bits, lengths, tile_index, rates, residues, freqs, gates, hist_hbm, w_hbm, out,
           hist, h_sem, w, w_sem, xs, pars, acc, term, got, flat, scale, full, part, got2, final,
           s1, r1, s2, r2, s3, r3):
    me, tm = lax.axis_index("seq"), lax.axis_index("tensor")
    blocks, layers, genomes = term.shape[:3]
    rows_dev = gates.shape[2]
    own_rows = layers * genomes * rows_dev
    cols = w.shape[2]
    wide_cols = SUB * LANE
    barrier = pltpu.get_barrier_semaphore()
    for k in range(1, seq):
        pl.semaphore_signal(barrier, inc=1, device_id={"seq": lax.rem(me + k, seq)}, device_id_type=MESH)
    for k in range(1, tensor):
        pl.semaphore_signal(barrier, inc=1, device_id={"tensor": lax.rem(tm + k, tensor)}, device_id_type=MESH)

    def load(c, l):
        return pltpu.make_async_copy(
            hist_hbm.at[l, :, :, pl.ds(pl.multiple_of(c * wide_cols, wide_cols), wide_cols)],
            hist.at[c, l], h_sem.at[c, l])

    for c in range(blocks):
        for l in range(layers):
            load(c, l).start()
    fetch = pltpu.make_async_copy(w_hbm, w, w_sem)
    fetch.start()
    tile = rows_dev * seq
    starts = [lengths[g] + tile * tile_index[0] for g in range(genomes)]
    first = me * hist.shape[3]
    for l in range(layers):
        for g in range(genomes):
            scale[pl.ds((l * genomes + g) * rows_dev, rows_dev), :] = gates[l, g].astype(jnp.float32)

    def rows_out(c, l, k):
        peer = lax.rem(me + k, seq)
        return pltpu.make_async_remote_copy(
            src_ref=term.at[c, l, :, peer], dst_ref=got.at[c, l, k],
            send_sem=s1.at[c, l, k], recv_sem=r1.at[c, l, k],
            device_id={"seq": peer}, device_id_type=MESH)

    def gated_out(c, k, src):
        return pltpu.make_async_remote_copy(
            src_ref=full.at[c, src], dst_ref=full.at[c, src], send_sem=s2.at[c, k], recv_sem=r2.at[c, k],
            device_id={"seq": lax.rem(me + k, seq)}, device_id_type=MESH)

    def gate(c):
        count = rows_dev * SUB
        for l in range(layers):
            for k in range(1, seq):
                rows_out(c, l, k).wait_recv()
            for g in range(genomes):
                total = term[c, l, g, me].astype(jnp.float32)
                for k in range(1, seq):
                    total = total + got[c, l, k, g].astype(jnp.float32)
                flat[pl.ds((l * genomes + g) * count, count), :] = total.reshape(count, LANE)
        for k in range(SUB):
            value = flat[pl.ds(k, own_rows, stride=SUB), :] * scale[:, pl.ds((c * SUB + k) * LANE, LANE)]
            full[c, me, :, pl.ds(k * LANE, LANE)] = value.astype(full.dtype)
        for k in range(1, seq):
            gated_out(c, k, me).start()

    @pl.loop(0, blocks * layers)
    def _(step):
        c, l = step // layers, step % layers
        load(c, l).wait()
        local_step(granule, bits, first, starts, hist.at[c, l], (rates, residues, freqs), l, c, acc, xs, pars)
        term[c, l] = acc[...].reshape(term.shape[2:]).astype(term.dtype)

        @pl.when(step == 0)
        def _():
            pl.semaphore_wait(barrier, seq + tensor - 2)

        for k in range(1, seq):
            rows_out(c, l, k).start()
        for done in range(blocks - 1):
            @pl.when(step == (done + 1) * layers)
            def _():
                gate(done)

    fetch.wait()
    share = seq // tensor
    wide = part.shape[3]
    per = tensor if seq * own_rows <= 256 else 1

    def project(c, n):
        @pl.loop(0, tensor // per)
        def _(t):
            block = full[c, pl.ds(t * (per * share), per * share)].reshape(per * share * own_rows, wide_cols)
            both = [jnp.dot(block, w[l, pl.ds(c * wide_cols, wide_cols), n * wide:(n + 1) * wide],
                            preferred_element_type=jnp.float32) for l in range(layers)]
            at = lax.broadcasted_iota(jnp.int32, both[0].shape, 0)
            owner = lax.rem(at, own_rows) // (own_rows // layers)
            value = both[0]
            for l in range(1, layers):
                value = jnp.where(owner == l, both[l], value)
            value = value.reshape(per, share * own_rows, wide)
            where = pl.ds(t * per, per)
            part[n, where] = value if c == 0 else part[n, where] + value

    def gathered(c):
        for k in range(1, seq):
            gated_out(c, k, lax.rem(me - k + seq, seq)).wait_recv()

    def shares_out(n, k):
        peer = lax.rem(tm + k, tensor)
        return pltpu.make_async_remote_copy(
            src_ref=part.at[n, peer], dst_ref=got2.at[n, k], send_sem=s3.at[n, k], recv_sem=r3.at[n, k],
            device_id={"tensor": peer}, device_id_type=MESH)

    chunks = cols // wide
    for c in range(blocks - 1):
        gathered(c)
        for n in range(chunks):
            project(c, n)
    gate(blocks - 1)
    gathered(blocks - 1)
    for n in range(chunks):
        project(blocks - 1, n)
        for k in range(1, tensor):
            shares_out(n, k).start()
    for n in range(chunks):
        total = part[n, tm]
        for k in range(1, tensor):
            shares_out(n, k).wait_recv()
            total = total + got2[n, k]
        for o in range(share):
            for l in range(layers):
                for g in range(genomes):
                    at = o * own_rows + (l * genomes + g) * rows_dev
                    final[l, g, o * rows_dev:(o + 1) * rows_dev, n * wide:(n + 1) * wide] = total[at:at + rows_dev]
    out[...] = final[...].astype(out.dtype)
    for k in range(1, seq):
        for c in range(blocks):
            for l in range(layers):
                rows_out(c, l, k).wait_send()
            gated_out(c, k, me).wait_send()
    for k in range(1, tensor):
        for n in range(chunks):
            shares_out(n, k).wait_send()


def shards(history, gates, rates, residues, freqs, w_out, lengths, tile_index):
    layers, genomes, span, chans = history.shape
    rows_dev = gates.shape[2]
    seq, tensor = lax.axis_size("seq"), lax.axis_size("tensor")
    tile = rows_dev * seq
    granule = math.gcd(UNIT, tile)
    bits = (span * seq // granule).bit_length()
    modes = rates.shape[1]
    wide_cols = SUB * LANE
    blocks = chans // wide_cols
    own_rows = layers * genomes * rows_dev
    cols = w_out.shape[2]
    wide = min(cols, 256)
    share = seq // tensor
    vmem = pl.BlockSpec(memory_space=pltpu.VMEM)
    smem = pl.BlockSpec(memory_space=pltpu.SMEM)
    hbm = pl.BlockSpec(memory_space=pl.ANY)
    piece = (rows_dev // 2, 2 * SUB, LANE)
    dma = pltpu.SemaphoreType.DMA
    return pl.pallas_call(
        functools.partial(kernel, seq, tensor, granule, bits),
        out_shape=jax.ShapeDtypeStruct((layers, genomes, share * rows_dev, cols), jnp.bfloat16),
        in_specs=[smem, smem, vmem, vmem, vmem, vmem, hbm, hbm],
        out_specs=vmem,
        scratch_shapes=[
            pltpu.VMEM((blocks, layers, genomes, span, wide_cols), history.dtype),
            dma((blocks, layers)),
            pltpu.VMEM(w_out.shape, w_out.dtype),
            dma,
            pltpu.VMEM((genomes, span * SUB, LANE), jnp.float32),
            pltpu.VMEM((3, modes * SUB, LANE), jnp.float32),
            pltpu.VMEM((genomes, tile, SUB, LANE), jnp.float32),
            pltpu.VMEM((blocks, layers, genomes, seq) + piece, jnp.bfloat16),
            pltpu.VMEM((blocks, layers, seq, genomes) + piece, jnp.bfloat16),
            pltpu.VMEM((own_rows * SUB, LANE), jnp.float32),
            pltpu.VMEM((own_rows, chans), jnp.float32),
            pltpu.VMEM((blocks, seq, own_rows, wide_cols), jnp.bfloat16),
            pltpu.VMEM((cols // wide, tensor, share * own_rows, wide), jnp.float32),
            pltpu.VMEM((cols // wide, tensor, share * own_rows, wide), jnp.float32),
            pltpu.VMEM((layers, genomes, share * rows_dev, cols), jnp.float32),
            dma((blocks, layers, seq)), dma((blocks, layers, seq)),
            dma((blocks, seq)), dma((blocks, seq)),
            dma((cols // wide, tensor)), dma((cols // wide, tensor)),
        ],
        compiler_params=pltpu.CompilerParams(
            collective_id=0, has_side_effects=True, vmem_limit_bytes=60 * 1024 * 1024),
    )(lengths, tile_index, rates, residues, freqs, gates, history, w_out)


def solution(mesh):
    in_specs = (
        P(None, None, "seq", "tensor"),
        P(None, None, "seq", "tensor"),
        P(None, None, "tensor"),
        P(None, None, "tensor"),
        P(None, None, "tensor"),
        P(None, "tensor", "seq"),
        P(),
        P(),
    )
    out_specs = P(None, None, "tensor", "seq")
    return jax.shard_map(shards, mesh=mesh, in_specs=in_specs, out_specs=out_specs, check_vma=False)
```

```python
import functools
import math

import jax
import jax.numpy as jnp
from jax import lax
from jax.experimental import pallas as pl
from jax.experimental.pallas import tpu as pltpu
from jax.sharding import PartitionSpec as P

MESH = pl.DeviceIdType.MESH
UNIT = 128
SUB = 8
LANE = 128
GROUP = 4
STEPS = 32
RUN = 32


def cmul(ar, ai, br, bi):
    return ar * br - ai * bi, ar * bi + ai * br


def csq(ar, ai):
    return ar * ar - ai * ai, 2.0 * (ar * ai)


def cos_sin(angle):
    y = (angle - 1.57079637050628662) + 4.37113883e-8
    y2 = y * y
    s = jnp.full_like(y, 1.0 / math.factorial(13))
    for n, sign in ((11, -1), (9, 1), (7, -1), (5, 1), (3, -1), (1, 1)):
        s = s * y2 + sign / math.factorial(n)
    c = jnp.full_like(y, -1.0 / math.factorial(14))
    for n, sign in ((12, 1), (10, -1), (8, 1), (6, -1), (4, 1), (2, -1), (0, 1)):
        c = c * y2 + sign / math.factorial(n)
    return -(s * y), c


def spread_rows(dst, base, value):
    count = value.shape[0]
    for k in range(SUB):
        dst[pl.ds(base + k, count, stride=SUB), :] = value[:, k * LANE:(k + 1) * LANE]


def local_step(granule, bits, first, starts, x_ref, params, l, c, acc, xs, pars):
    genomes, span = x_ref.shape[:2]
    modes = params[0].shape[1]
    rows = acc.shape[1]
    chunk = 32
    wide_cols = SUB * LANE
    for i, ref in enumerate(params):
        spread_rows(pars.at[i], 0, ref[l, :, pl.ds(pl.multiple_of(c * wide_cols, wide_cols), wide_cols)])
    hops, blocks_live = [], []
    for g in range(genomes):
        ahead = jnp.full((SUB, LANE), starts[g] - first, jnp.int32)
        live = jnp.minimum(jnp.maximum(ahead, 0), span)
        blocks_live.append(live)
        hops.append(jnp.maximum(ahead - live, 0))

        @pl.loop(0, span // chunk)
        def _(q):
            block = x_ref[g, pl.ds(pl.multiple_of(q * chunk, chunk), chunk), :]
            spread_rows(xs.at[g], q * (chunk * SUB), block.astype(jnp.float32))

    acc[...] = jnp.zeros_like(acc)
    wide = GROUP * SUB

    @pl.loop(0, modes // GROUP)
    def _(mg):
        at = pl.ds(pl.multiple_of(mg * wide, wide), wide)
        rate, resid, freq = pars[0, at, :], pars[1, at, :], pars[2, at, :]
        decay = jnp.exp(-rate)
        c, s = cos_sin(freq)
        zr, zi = decay * c, decay * s
        trace, norm = 2.0 * zr, zr * zr + zi * zi
        amp = resid * jnp.sqrt(rate)

        def cut(v):
            return [v[i * SUB:(i + 1) * SUB] for i in range(GROUP)]

        zr_c, zi_c, tr_c, no_c = cut(zr), cut(zi), cut(trace), cut(norm)
        pr, pi = zr, zi
        for _ in range(int(math.log2(STEPS))):
            pr, pi = csq(pr, pi)
        br_c, bi_c = cut(pr), cut(pi)
        n_state = genomes * GROUP
        zero = jnp.zeros((SUB, LANE), jnp.float32)

        def block_step(blk, carry):
            re, im = carry
            a = [zero] * n_state
            b = [zero] * n_state
            for t in range(STEPS):
                for g in range(genomes):
                    x = xs[g, pl.ds(pl.multiple_of(blk * (STEPS * SUB) + t * SUB, SUB), SUB), :]
                    for i in range(GROUP):
                        k = g * GROUP + i
                        a[k], b[k] = b[k] + tr_c[i] * a[k], x - no_c[i] * a[k]
            new_re, new_im = [], []
            for g in range(genomes):
                for i in range(GROUP):
                    k = g * GROUP + i
                    sr, si = cmul(br_c[i], bi_c[i], re[k], im[k])
                    keep = blocks_live[g] > blk * STEPS
                    new_re.append(jnp.where(keep, sr + (zr_c[i] * a[k] + b[k]), re[k]))
                    new_im.append(jnp.where(keep, si + zi_c[i] * a[k], im[k]))
            return tuple(new_re), tuple(new_im)

        init = ((zero,) * n_state, (zero,) * n_state)
        re, im = lax.fori_loop(0, span // STEPS, block_step, init)

        pr, pi = zr, zi
        for _ in range(int(math.log2(granule))):
            pr, pi = csq(pr, pi)
        lead_r, lead_i = amp * zr, amp * zi
        far_r = [cut(lead_r) for _ in range(genomes)]
        far_i = [cut(lead_i) for _ in range(genomes)]
        for bit in range(bits):
            pr_c, pi_c = cut(pr), cut(pi)
            for g in range(genomes):
                on = (hops[g] & (granule << bit)) != 0
                for i in range(GROUP):
                    nr, ni = cmul(far_r[g][i], far_i[g][i], pr_c[i], pi_c[i])
                    far_r[g][i] = jnp.where(on, nr, far_r[g][i])
                    far_i[g][i] = jnp.where(on, ni, far_i[g][i])
            if bit + 1 < bits:
                pr, pi = csq(pr, pi)
        start = []
        for g in range(genomes):
            fr, fi = far_r[g], far_i[g]
            start.append([cmul(re[g * GROUP + i], im[g * GROUP + i], fr[i], fi[i]) for i in range(GROUP)])
        qr, qi = zr, zi
        for _ in range(int(math.log2(RUN))):
            qr, qi = csq(qr, qi)
        qr_c, qi_c = cut(qr), cut(qi)

        def row_run(run, carry):
            wr, wi = carry
            base = run * RUN
            old = [None] * n_state
            now = list(wr)
            for j in range(RUN):
                for g in range(genomes):
                    total = now[g * GROUP]
                    for i in range(1, GROUP):
                        total = total + now[g * GROUP + i]
                    acc[g, base + j] += total
                for g in range(genomes):
                    for i in range(GROUP):
                        k = g * GROUP + i
                        if j == 0:
                            nxt = wr[k] * zr_c[i] - wi[k] * zi_c[i]
                        else:
                            nxt = tr_c[i] * now[k] - no_c[i] * old[k]
                        old[k], now[k] = now[k], nxt
            moved = [cmul(wr[g * GROUP + i], wi[g * GROUP + i], qr_c[i], qi_c[i])
                     for g in range(genomes) for i in range(GROUP)]
            return tuple(m[0] for m in moved), tuple(m[1] for m in moved)

        wr = tuple(start[g][i][0] for g in range(genomes) for i in range(GROUP))
        wi = tuple(start[g][i][1] for g in range(genomes) for i in range(GROUP))
        lax.fori_loop(0, rows // RUN, row_run, (wr, wi))


def kernel(seq, tensor, granule, bits, lengths, tile_index, rates, residues, freqs, gates, hist_hbm, w_hbm, out,
           hist, h_sem, w, w_sem, xs, pars, acc, term, got, flat, folded, scale, full, part, got2, final,
           s1, r1, s2, r2, s3, r3):
    me, tm = lax.axis_index("seq"), lax.axis_index("tensor")
    blocks, layers, genomes = term.shape[:3]
    rows_dev = gates.shape[2]
    own_rows = layers * genomes * rows_dev
    cols = w.shape[2]
    wide_cols = SUB * LANE
    barrier = pltpu.get_barrier_semaphore()
    for k in range(1, seq):
        pl.semaphore_signal(barrier, inc=1, device_id={"seq": lax.rem(me + k, seq)}, device_id_type=MESH)
    for k in range(1, tensor):
        pl.semaphore_signal(barrier, inc=1, device_id={"tensor": lax.rem(tm + k, tensor)}, device_id_type=MESH)

    def load(c, l):
        return pltpu.make_async_copy(
            hist_hbm.at[l, :, :, pl.ds(pl.multiple_of(c * wide_cols, wide_cols), wide_cols)],
            hist.at[c, l], h_sem.at[c, l])

    for c in range(blocks):
        for l in range(layers):
            load(c, l).start()
    fetch = pltpu.make_async_copy(w_hbm, w, w_sem)
    fetch.start()
    tile = rows_dev * seq
    starts = [lengths[g] + tile * tile_index[0] for g in range(genomes)]
    first = me * hist.shape[3]
    for l in range(layers):
        for g in range(genomes):
            scale[pl.ds((l * genomes + g) * rows_dev, rows_dev), :] = gates[l, g].astype(jnp.float32)

    def rows_out(c, l, k):
        peer = lax.rem(me + k, seq)
        return pltpu.make_async_remote_copy(
            src_ref=term.at[c, l, :, peer], dst_ref=got.at[c, l, k],
            send_sem=s1.at[c, l, k], recv_sem=r1.at[c, l, k],
            device_id={"seq": peer}, device_id_type=MESH)

    def gated_out(c, l, k, src):
        return pltpu.make_async_remote_copy(
            src_ref=full.at[c, l, src], dst_ref=full.at[c, l, src],
            send_sem=s2.at[c, l, k], recv_sem=r2.at[c, l, k],
            device_id={"seq": lax.rem(me + k, seq)}, device_id_type=MESH)

    layer_rows = genomes * rows_dev
    fold = SUB // 2

    def gate(c, l):
        count = rows_dev * SUB
        for k in range(1, seq):
            rows_out(c, l, k).wait_recv()
        for g in range(genomes):
            total = term[c, l, g, me].astype(jnp.float32)
            for k in range(1, seq):
                total = total + got[c, l, k, g].astype(jnp.float32)
            flat[pl.ds(g * count, count), :] = total.reshape(count, LANE)
        for k in range(SUB):
            at = pl.ds(pl.multiple_of(l * layer_rows, layer_rows), layer_rows)
            lanes = pl.ds(pl.multiple_of((c * SUB + k) * LANE, LANE), LANE)
            value = flat[pl.ds(k, layer_rows, stride=SUB), :] * scale[at, lanes]
            folded[pl.ds(k // fold * layer_rows, layer_rows), pl.ds(k % fold * LANE, LANE)] = value
        full[c, l, me] = folded[...].astype(full.dtype)
        for k in range(1, seq):
            gated_out(c, l, k, me).start()

    @pl.loop(0, blocks * layers)
    def _(step):
        c, l = step // layers, step % layers
        load(c, l).wait()
        local_step(granule, bits, first, starts, hist.at[c, l], (rates, residues, freqs), l, c, acc, xs, pars)
        term[c, l] = acc[...].reshape(term.shape[2:]).astype(term.dtype)

        @pl.when(step == 0)
        def _():
            pl.semaphore_wait(barrier, seq + tensor - 2)

        for k in range(1, seq):
            rows_out(c, l, k).start()

        @pl.when(step > 0)
        def _():
            gate((step - 1) // layers, (step - 1) % layers)

    fetch.wait()
    share = seq // tensor
    wide = part.shape[4]
    per = tensor if 2 * seq * layer_rows <= 256 else 1
    depth = fold * LANE

    def project(c, l, n):
        @pl.loop(0, tensor // per)
        def _(t):
            block = full[c, l, pl.ds(t * (per * share), per * share)].reshape(per * share * 2 * layer_rows, depth)
            value = 0.0
            for h in range(2):
                both = jnp.dot(block, w[l, pl.ds(c * wide_cols + h * depth, depth), n * wide:(n + 1) * wide],
                               preferred_element_type=jnp.float32)
                value = value + both.reshape(per * share, 2, layer_rows, wide)[:, h]
            value = value.reshape(per, share * layer_rows, wide)
            where = pl.ds(t * per, per)
            part[l, n, where] = value if c == 0 else part[l, n, where] + value

    def gathered(c, l):
        for k in range(1, seq):
            gated_out(c, l, k, lax.rem(me - k + seq, seq)).wait_recv()

    def shares_out(l, n, k):
        peer = lax.rem(tm + k, tensor)
        return pltpu.make_async_remote_copy(
            src_ref=part.at[l, n, peer], dst_ref=got2.at[l, n, k], send_sem=s3.at[l, n, k], recv_sem=r3.at[l, n, k],
            device_id={"tensor": peer}, device_id_type=MESH)

    chunks = cols // wide
    order = [(c, l) for c in range(blocks) for l in range(layers)]

    def advance(c, l):
        gathered(c, l)
        for n in range(chunks):
            project(c, l, n)
            if c == blocks - 1:
                for k in range(1, tensor):
                    shares_out(l, n, k).start()

    for c, l in order[:-2]:
        advance(c, l)
    gate(*order[-1])
    for c, l in order[-2:]:
        advance(c, l)
    for l in range(layers):
        for n in range(chunks):
            total = part[l, n, tm]
            for k in range(1, tensor):
                shares_out(l, n, k).wait_recv()
                total = total + got2[l, n, k]
            for o in range(share):
                for g in range(genomes):
                    at = o * layer_rows + g * rows_dev
                    final[l, g, o * rows_dev:(o + 1) * rows_dev, n * wide:(n + 1) * wide] = total[at:at + rows_dev]
    out[...] = final[...].astype(out.dtype)
    for c, l in order:
        for k in range(1, seq):
            rows_out(c, l, k).wait_send()
            gated_out(c, l, k, me).wait_send()
    for l in range(layers):
        for n in range(chunks):
            for k in range(1, tensor):
                shares_out(l, n, k).wait_send()


def shards(history, gates, rates, residues, freqs, w_out, lengths, tile_index):
    layers, genomes, span, chans = history.shape
    rows_dev = gates.shape[2]
    seq, tensor = lax.axis_size("seq"), lax.axis_size("tensor")
    tile = rows_dev * seq
    granule = math.gcd(UNIT, tile)
    bits = (span * seq // granule).bit_length()
    modes = rates.shape[1]
    wide_cols = SUB * LANE
    blocks = chans // wide_cols
    own_rows = layers * genomes * rows_dev
    cols = w_out.shape[2]
    wide = min(cols, 256)
    share = seq // tensor
    vmem = pl.BlockSpec(memory_space=pltpu.VMEM)
    smem = pl.BlockSpec(memory_space=pltpu.SMEM)
    hbm = pl.BlockSpec(memory_space=pl.ANY)
    piece = (rows_dev // 2, 2 * SUB, LANE)
    dma = pltpu.SemaphoreType.DMA
    return pl.pallas_call(
        functools.partial(kernel, seq, tensor, granule, bits),
        out_shape=jax.ShapeDtypeStruct((layers, genomes, share * rows_dev, cols), jnp.bfloat16),
        in_specs=[smem, smem, vmem, vmem, vmem, vmem, hbm, hbm],
        out_specs=vmem,
        scratch_shapes=[
            pltpu.VMEM((blocks, layers, genomes, span, wide_cols), history.dtype),
            dma((blocks, layers)),
            pltpu.VMEM(w_out.shape, w_out.dtype),
            dma,
            pltpu.VMEM((genomes, span * SUB, LANE), jnp.float32),
            pltpu.VMEM((3, modes * SUB, LANE), jnp.float32),
            pltpu.VMEM((genomes, tile, SUB, LANE), jnp.float32),
            pltpu.VMEM((blocks, layers, genomes, seq) + piece, jnp.bfloat16),
            pltpu.VMEM((blocks, layers, seq, genomes) + piece, jnp.bfloat16),
            pltpu.VMEM((genomes * rows_dev * SUB, LANE), jnp.float32),
            pltpu.VMEM((2 * genomes * rows_dev, wide_cols // 2), jnp.float32),
            pltpu.VMEM((own_rows, chans), jnp.float32),
            pltpu.VMEM((blocks, layers, seq, 2 * genomes * rows_dev, wide_cols // 2), jnp.bfloat16),
            pltpu.VMEM((layers, cols // wide, tensor, share * genomes * rows_dev, wide), jnp.float32),
            pltpu.VMEM((layers, cols // wide, tensor, share * genomes * rows_dev, wide), jnp.float32),
            pltpu.VMEM((layers, genomes, share * rows_dev, cols), jnp.float32),
            dma((blocks, layers, seq)), dma((blocks, layers, seq)),
            dma((blocks, layers, seq)), dma((blocks, layers, seq)),
            dma((layers, cols // wide, tensor)), dma((layers, cols // wide, tensor)),
        ],
        compiler_params=pltpu.CompilerParams(
            collective_id=0, has_side_effects=True, vmem_limit_bytes=60 * 1024 * 1024),
    )(lengths, tile_index, rates, residues, freqs, gates, history, w_out)


def solution(mesh):
    in_specs = (
        P(None, None, "seq", "tensor"),
        P(None, None, "seq", "tensor"),
        P(None, None, "tensor"),
        P(None, None, "tensor"),
        P(None, None, "tensor"),
        P(None, "tensor", "seq"),
        P(),
        P(),
    )
    out_specs = P(None, None, "tensor", "seq")
    return jax.shard_map(shards, mesh=mesh, in_specs=in_specs, out_specs=out_specs, check_vma=False)
```

```python
import functools
import math

import jax
import jax.numpy as jnp
from jax import lax
from jax.experimental import pallas as pl
from jax.experimental.pallas import tpu as pltpu
from jax.sharding import PartitionSpec as P

MESH = pl.DeviceIdType.MESH
UNIT = 128
SUB = 8
LANE = 128
GROUP = 4
STEPS = 64
RUN = 32


def cmul(ar, ai, br, bi):
    return ar * br - ai * bi, ar * bi + ai * br


def csq(ar, ai):
    return ar * ar - ai * ai, 2.0 * (ar * ai)


def cos_sin(angle):
    y = (angle - 1.57079637050628662) + 4.37113883e-8
    y2 = y * y
    s = jnp.full_like(y, 1.0 / math.factorial(13))
    for n, sign in ((11, -1), (9, 1), (7, -1), (5, 1), (3, -1), (1, 1)):
        s = s * y2 + sign / math.factorial(n)
    c = jnp.full_like(y, -1.0 / math.factorial(14))
    for n, sign in ((12, 1), (10, -1), (8, 1), (6, -1), (4, 1), (2, -1), (0, 1)):
        c = c * y2 + sign / math.factorial(n)
    return -(s * y), c


def spread_rows(dst, base, value):
    count = value.shape[0]
    for k in range(SUB):
        dst[pl.ds(base + k, count, stride=SUB), :] = value[:, k * LANE:(k + 1) * LANE]


def local_step(granule, bits, first, starts, x_ref, params, l, c, acc, xs, pars):
    genomes, span = x_ref.shape[:2]
    modes = params[0].shape[1]
    rows = acc.shape[1]
    chunk = STEPS // 2
    wide_cols = SUB * LANE
    for i, ref in enumerate(params):
        spread_rows(pars.at[i], 0, ref[l, :, pl.ds(pl.multiple_of(c * wide_cols, wide_cols), wide_cols)])
    hops, blocks_live = [], []
    for g in range(genomes):
        ahead = jnp.full((SUB, LANE), starts[g] - first, jnp.int32)
        live = jnp.minimum(jnp.maximum(ahead, 0), span)
        blocks_live.append(live + (live & chunk))
        count = jnp.minimum(jnp.maximum(starts[g] - first, 0), span)
        odd = (jnp.full((chunk, wide_cols), count, jnp.int32) & chunk) != 0
        hops.append(jnp.maximum(ahead - live, 0))

        @pl.loop(0, span // chunk)
        def _(q):
            block = x_ref[g, pl.ds(pl.multiple_of(q * chunk, chunk), chunk), :]
            before = x_ref[g, pl.ds(pl.multiple_of(jnp.maximum(q - 1, 0) * chunk, chunk), chunk), :]
            before = before.astype(jnp.float32) * jnp.minimum(q, 1).astype(jnp.float32)
            spread_rows(xs.at[g], q * (chunk * SUB), jnp.where(odd, before, block.astype(jnp.float32)))

    acc[...] = jnp.zeros_like(acc)
    wide = GROUP * SUB

    @pl.loop(0, modes // GROUP)
    def _(mg):
        at = pl.ds(pl.multiple_of(mg * wide, wide), wide)
        rate, resid, freq = pars[0, at, :], pars[1, at, :], pars[2, at, :]
        decay = jnp.exp(-rate)
        c, s = cos_sin(freq)
        zr, zi = decay * c, decay * s
        trace, norm = 2.0 * zr, zr * zr + zi * zi
        amp = resid * jnp.sqrt(rate)

        def cut(v):
            return [v[i * SUB:(i + 1) * SUB] for i in range(GROUP)]

        zr_c, zi_c, tr_c, no_c = cut(zr), cut(zi), cut(trace), cut(norm)
        pr, pi = zr, zi
        for _ in range(int(math.log2(STEPS))):
            pr, pi = csq(pr, pi)
        br_c, bi_c = cut(pr), cut(pi)
        n_state = genomes * GROUP
        zero = jnp.zeros((SUB, LANE), jnp.float32)

        def block_step(blk, carry):
            re, im = carry
            a = [zero] * n_state
            b = [zero] * n_state
            for t in range(STEPS):
                for g in range(genomes):
                    x = xs[g, pl.ds(pl.multiple_of(blk * (STEPS * SUB) + t * SUB, SUB), SUB), :]
                    for i in range(GROUP):
                        k = g * GROUP + i
                        a[k], b[k] = b[k] + tr_c[i] * a[k], x - no_c[i] * a[k]
            new_re, new_im = [], []
            for g in range(genomes):
                for i in range(GROUP):
                    k = g * GROUP + i
                    sr, si = cmul(br_c[i], bi_c[i], re[k], im[k])
                    keep = blocks_live[g] > blk * STEPS
                    new_re.append(jnp.where(keep, sr + (zr_c[i] * a[k] + b[k]), re[k]))
                    new_im.append(jnp.where(keep, si + zi_c[i] * a[k], im[k]))
            return tuple(new_re), tuple(new_im)

        init = ((zero,) * n_state, (zero,) * n_state)
        re, im = lax.fori_loop(0, span // STEPS, block_step, init)

        pr, pi = zr, zi
        for _ in range(int(math.log2(granule))):
            pr, pi = csq(pr, pi)
        lead_r, lead_i = amp * zr, amp * zi
        far_r = [cut(lead_r) for _ in range(genomes)]
        far_i = [cut(lead_i) for _ in range(genomes)]
        for bit in range(bits):
            pr_c, pi_c = cut(pr), cut(pi)
            for g in range(genomes):
                on = (hops[g] & (granule << bit)) != 0
                for i in range(GROUP):
                    nr, ni = cmul(far_r[g][i], far_i[g][i], pr_c[i], pi_c[i])
                    far_r[g][i] = jnp.where(on, nr, far_r[g][i])
                    far_i[g][i] = jnp.where(on, ni, far_i[g][i])
            if bit + 1 < bits:
                pr, pi = csq(pr, pi)
        start = []
        for g in range(genomes):
            fr, fi = far_r[g], far_i[g]
            start.append([cmul(re[g * GROUP + i], im[g * GROUP + i], fr[i], fi[i]) for i in range(GROUP)])
        qr, qi = zr, zi
        for _ in range(int(math.log2(RUN))):
            qr, qi = csq(qr, qi)
        qr_c, qi_c = cut(qr), cut(qi)

        def row_run(run, carry):
            wr, wi = carry
            base = run * RUN
            old = [None] * n_state
            now = list(wr)
            for j in range(RUN):
                for g in range(genomes):
                    total = now[g * GROUP]
                    for i in range(1, GROUP):
                        total = total + now[g * GROUP + i]
                    acc[g, base + j] += total
                for g in range(genomes):
                    for i in range(GROUP):
                        k = g * GROUP + i
                        if j == 0:
                            nxt = wr[k] * zr_c[i] - wi[k] * zi_c[i]
                        else:
                            nxt = tr_c[i] * now[k] - no_c[i] * old[k]
                        old[k], now[k] = now[k], nxt
            moved = [cmul(wr[g * GROUP + i], wi[g * GROUP + i], qr_c[i], qi_c[i])
                     for g in range(genomes) for i in range(GROUP)]
            return tuple(m[0] for m in moved), tuple(m[1] for m in moved)

        wr = tuple(start[g][i][0] for g in range(genomes) for i in range(GROUP))
        wi = tuple(start[g][i][1] for g in range(genomes) for i in range(GROUP))
        lax.fori_loop(0, rows // RUN, row_run, (wr, wi))


def kernel(seq, tensor, granule, bits, lengths, tile_index, rates, residues, freqs, gates, hist_hbm, w_hbm, out,
           hist, h_sem, w, w_sem, xs, pars, acc, term, got, flat, folded, scale, full, part, got2, final,
           s1, r1, s2, r2, s3, r3):
    me, tm = lax.axis_index("seq"), lax.axis_index("tensor")
    blocks, layers, genomes = term.shape[:3]
    rows_dev = gates.shape[2]
    own_rows = layers * genomes * rows_dev
    cols = w.shape[2]
    wide_cols = SUB * LANE
    barrier = pltpu.get_barrier_semaphore()
    for k in range(1, seq):
        pl.semaphore_signal(barrier, inc=1, device_id={"seq": lax.rem(me + k, seq)}, device_id_type=MESH)
    for k in range(1, tensor):
        pl.semaphore_signal(barrier, inc=1, device_id={"tensor": lax.rem(tm + k, tensor)}, device_id_type=MESH)

    def load(c, l):
        return pltpu.make_async_copy(
            hist_hbm.at[l, :, :, pl.ds(pl.multiple_of(c * wide_cols, wide_cols), wide_cols)],
            hist.at[c, l], h_sem.at[c, l])

    for c in range(blocks):
        for l in range(layers):
            load(c, l).start()
    fetch = pltpu.make_async_copy(w_hbm, w, w_sem)
    fetch.start()
    tile = rows_dev * seq
    starts = [lengths[g] + tile * tile_index[0] for g in range(genomes)]
    first = me * hist.shape[3]
    for l in range(layers):
        for g in range(genomes):
            scale[pl.ds((l * genomes + g) * rows_dev, rows_dev), :] = gates[l, g].astype(jnp.float32)

    def rows_out(c, l, k):
        peer = lax.rem(me + k, seq)
        return pltpu.make_async_remote_copy(
            src_ref=term.at[c, l, :, peer], dst_ref=got.at[c, l, k],
            send_sem=s1.at[c, l, k], recv_sem=r1.at[c, l, k],
            device_id={"seq": peer}, device_id_type=MESH)

    def gated_out(c, l, k, src):
        return pltpu.make_async_remote_copy(
            src_ref=full.at[c, l, src], dst_ref=full.at[c, l, src],
            send_sem=s2.at[c, l, k], recv_sem=r2.at[c, l, k],
            device_id={"seq": lax.rem(me + k, seq)}, device_id_type=MESH)

    layer_rows = genomes * rows_dev
    fold = SUB // 2

    def gate(c, l):
        count = rows_dev * SUB
        for k in range(1, seq):
            rows_out(c, l, k).wait_recv()
        for g in range(genomes):
            total = term[c, l, g, me].astype(jnp.float32)
            for k in range(1, seq):
                total = total + got[c, l, k, g].astype(jnp.float32)
            flat[pl.ds(g * count, count), :] = total.reshape(count, LANE)
        for k in range(SUB):
            at = pl.ds(pl.multiple_of(l * layer_rows, layer_rows), layer_rows)
            lanes = pl.ds(pl.multiple_of((c * SUB + k) * LANE, LANE), LANE)
            value = flat[pl.ds(k, layer_rows, stride=SUB), :] * scale[at, lanes]
            folded[pl.ds(k // fold * layer_rows, layer_rows), pl.ds(k % fold * LANE, LANE)] = value
        full[c, l, me] = folded[...].astype(full.dtype)
        for k in range(1, seq):
            gated_out(c, l, k, me).start()

    @pl.loop(0, blocks * layers)
    def _(step):
        c, l = step // layers, step % layers
        load(c, l).wait()
        local_step(granule, bits, first, starts, hist.at[c, l], (rates, residues, freqs), l, c, acc, xs, pars)
        term[c, l] = acc[...].reshape(term.shape[2:]).astype(term.dtype)

        @pl.when(step == 0)
        def _():
            pl.semaphore_wait(barrier, seq + tensor - 2)

        for k in range(1, seq):
            rows_out(c, l, k).start()

        @pl.when(step > 0)
        def _():
            gate((step - 1) // layers, (step - 1) % layers)

    fetch.wait()
    share = seq // tensor
    wide = part.shape[4]
    per = tensor if 2 * seq * layer_rows <= 256 else 1
    depth = fold * LANE

    def project(c, l, n):
        @pl.loop(0, tensor // per)
        def _(t):
            block = full[c, l, pl.ds(t * (per * share), per * share)].reshape(per * share * 2 * layer_rows, depth)
            value = 0.0
            for h in range(2):
                both = jnp.dot(block, w[l, pl.ds(c * wide_cols + h * depth, depth), n * wide:(n + 1) * wide],
                               preferred_element_type=jnp.float32)
                value = value + both.reshape(per * share, 2, layer_rows, wide)[:, h]
            value = value.reshape(per, share * layer_rows, wide)
            where = pl.ds(t * per, per)
            part[l, n, where] = value if c == 0 else part[l, n, where] + value

    def gathered(c, l):
        for k in range(1, seq):
            gated_out(c, l, k, lax.rem(me - k + seq, seq)).wait_recv()

    def shares_out(l, n, k):
        peer = lax.rem(tm + k, tensor)
        return pltpu.make_async_remote_copy(
            src_ref=part.at[l, n, peer], dst_ref=got2.at[l, n, k], send_sem=s3.at[l, n, k], recv_sem=r3.at[l, n, k],
            device_id={"tensor": peer}, device_id_type=MESH)

    chunks = cols // wide
    order = [(c, l) for c in range(blocks) for l in range(layers)]

    def advance(c, l):
        gathered(c, l)
        for n in range(chunks):
            project(c, l, n)
            if c == blocks - 1:
                for k in range(1, tensor):
                    shares_out(l, n, k).start()

    for c, l in order[:-2]:
        advance(c, l)
    gate(*order[-1])
    for c, l in order[-2:]:
        advance(c, l)
    for l in range(layers):
        for n in range(chunks):
            total = part[l, n, tm]
            for k in range(1, tensor):
                shares_out(l, n, k).wait_recv()
                total = total + got2[l, n, k]
            for o in range(share):
                for g in range(genomes):
                    at = o * layer_rows + g * rows_dev
                    final[l, g, o * rows_dev:(o + 1) * rows_dev, n * wide:(n + 1) * wide] = total[at:at + rows_dev]
    out[...] = final[...].astype(out.dtype)
    for c, l in order:
        for k in range(1, seq):
            rows_out(c, l, k).wait_send()
            gated_out(c, l, k, me).wait_send()
    for l in range(layers):
        for n in range(chunks):
            for k in range(1, tensor):
                shares_out(l, n, k).wait_send()


def shards(history, gates, rates, residues, freqs, w_out, lengths, tile_index):
    layers, genomes, span, chans = history.shape
    rows_dev = gates.shape[2]
    seq, tensor = lax.axis_size("seq"), lax.axis_size("tensor")
    tile = rows_dev * seq
    granule = math.gcd(UNIT, tile)
    bits = (span * seq // granule).bit_length()
    modes = rates.shape[1]
    wide_cols = SUB * LANE
    blocks = chans // wide_cols
    own_rows = layers * genomes * rows_dev
    cols = w_out.shape[2]
    wide = min(cols, 256)
    share = seq // tensor
    vmem = pl.BlockSpec(memory_space=pltpu.VMEM)
    smem = pl.BlockSpec(memory_space=pltpu.SMEM)
    hbm = pl.BlockSpec(memory_space=pl.ANY)
    piece = (rows_dev // 2, 2 * SUB, LANE)
    dma = pltpu.SemaphoreType.DMA
    return pl.pallas_call(
        functools.partial(kernel, seq, tensor, granule, bits),
        out_shape=jax.ShapeDtypeStruct((layers, genomes, share * rows_dev, cols), jnp.bfloat16),
        in_specs=[smem, smem, vmem, vmem, vmem, vmem, hbm, hbm],
        out_specs=vmem,
        scratch_shapes=[
            pltpu.VMEM((blocks, layers, genomes, span, wide_cols), history.dtype),
            dma((blocks, layers)),
            pltpu.VMEM(w_out.shape, w_out.dtype),
            dma,
            pltpu.VMEM((genomes, span * SUB, LANE), jnp.float32),
            pltpu.VMEM((3, modes * SUB, LANE), jnp.float32),
            pltpu.VMEM((genomes, tile, SUB, LANE), jnp.float32),
            pltpu.VMEM((blocks, layers, genomes, seq) + piece, jnp.bfloat16),
            pltpu.VMEM((blocks, layers, seq, genomes) + piece, jnp.bfloat16),
            pltpu.VMEM((genomes * rows_dev * SUB, LANE), jnp.float32),
            pltpu.VMEM((2 * genomes * rows_dev, wide_cols // 2), jnp.float32),
            pltpu.VMEM((own_rows, chans), jnp.float32),
            pltpu.VMEM((blocks, layers, seq, 2 * genomes * rows_dev, wide_cols // 2), jnp.bfloat16),
            pltpu.VMEM((layers, cols // wide, tensor, share * genomes * rows_dev, wide), jnp.float32),
            pltpu.VMEM((layers, cols // wide, tensor, share * genomes * rows_dev, wide), jnp.float32),
            pltpu.VMEM((layers, genomes, share * rows_dev, cols), jnp.float32),
            dma((blocks, layers, seq)), dma((blocks, layers, seq)),
            dma((blocks, layers, seq)), dma((blocks, layers, seq)),
            dma((layers, cols // wide, tensor)), dma((layers, cols // wide, tensor)),
        ],
        compiler_params=pltpu.CompilerParams(
            collective_id=0, has_side_effects=True, vmem_limit_bytes=60 * 1024 * 1024),
    )(lengths, tile_index, rates, residues, freqs, gates, history, w_out)


def solution(mesh):
    in_specs = (
        P(None, None, "seq", "tensor"),
        P(None, None, "seq", "tensor"),
        P(None, None, "tensor"),
        P(None, None, "tensor"),
        P(None, None, "tensor"),
        P(None, "tensor", "seq"),
        P(),
        P(),
    )
    out_specs = P(None, None, "tensor", "seq")
    return jax.shard_map(shards, mesh=mesh, in_specs=in_specs, out_specs=out_specs, check_vma=False)
```
